128 devices in a mesh: ri: 16 (over z, y), ao: 8 (over x, core).
Axes of the slice: x: 4, y: 4, z: 4, core: 2. Of those that a mesh axis runs over, the one named last changes fastest.
Arguments:
- three_center: bfloat16 [64, 16, 4, 128, 128], P('ri', 'ao'), may hold values from -6 to 6
- neighbors: int32 [16, 4], P('ao'), may hold values from 0 to 15, as said below
- block_sizes: int32 [16], replicated, may hold values from 64 to 128
- green_occ: bfloat16 [2048, 2048], P(('ri', 'ao')), may hold values from -0.25 to 0.25
- green_virt: bfloat16 [2048, 2048], P(('ri', 'ao')), may hold values from -0.125 to 0.125
Outputs:
- contracted: float32 [64, 2048, 2048], P('ri', None, 'ao')
The draws below stay inside these ranges and needn't reach their ends.
Inputs may be any that keep to these rules, and one draw needn't show every extreme that they name: neighbors[a, 0] = a, and the 4 entries of a row differ.
All inputs are finite; a program needn't handle non-finite values.
Results may differ from the reference program's by a relative error of at most 0.0029.
Values may be sent and summed in bfloat16 or wider, within the bound.
No kernel may reach another device: no remote copies, remote signals or barrier semaphores. Data moves between devices by JAX's collectives and lax.ppermute only.
A program may use at most 128 MiB of HBM per device.

```python
import jax
import jax.numpy as jnp
from jax import lax

BS = 128
NBR = 4
RI = 64
NAT = 16
NAO = 2048


def draw_neighbors(key, part):
    key = jax.random.fold_in(key, 11)
    scores = jax.random.randint(key, (NAT, NAT), 0, 1 << 20)
    column = jnp.arange(NAT, dtype=jnp.int32)
    scores = scores * NAT + column[None, :]
    scores = jnp.where(column[None, :] == column[:, None], -1, scores)
    ordering = jnp.argsort(scores, axis=1, stable=True)
    return ordering[:, :NBR].astype(jnp.int32)


def draw_block_sizes(key, part):
    key = jax.random.fold_in(key, 23)
    key_sizes, key_first, key_second = jax.random.split(key, 3)
    sizes = jax.random.randint(key_sizes, (NAT,), BS // 2, BS + 1)
    largest = jax.random.randint(key_first, (), 0, NAT)
    smallest = (largest + 1 + jax.random.randint(key_second, (), 0, NAT - 1)) % NAT
    column = jnp.arange(NAT)
    sizes = jnp.where(column == largest, BS, jnp.where(column == smallest, BS // 2, sizes))
    return sizes.astype(jnp.int32)


def shard_levels(key, dims, shards, least, top_value):
    loudness, own = 1.0, jax.random.fold_in(key, 6)
    for axis_at, shards_of in shards:
        steps = jnp.exp(jax.random.uniform(jax.random.fold_in(own, axis_at), (shards_of,), jnp.float32, least / len(shards), top_value / len(shards)))
        loudness = loudness * jnp.repeat(steps, dims[axis_at] // shards_of).reshape([-1 if axis == axis_at else 1 for axis in range(len(dims))])
    return loudness


def noise(own_key, extent, spread, limit, cuts=(), held_as=jnp.bfloat16):
    loudness = shard_levels(own_key, extent, cuts, -0.22, 0.18) if cuts else 1.0
    entries = jax.random.normal(own_key, extent, jnp.float32) * spread * loudness
    return jnp.minimum(jnp.maximum(entries, -limit), limit).astype(held_as)


def setup_inputs(seed: int = 0) -> dict:
    seeds = jax.random.split(jax.random.key(seed), 6)
    return {
        "three_center": noise(seeds[0], (RI, NAT, NBR, BS, BS), 1.0, 6.0, ((0, 16), (1, 8))),
        "neighbors": draw_neighbors(jax.random.fold_in(seeds[5], 71), 0),
        "block_sizes": draw_block_sizes(jax.random.fold_in(seeds[5], 71), 0),
        "green_occ": noise(seeds[3], (NAO, NAO), (NBR * BS) ** -0.5, 0.25, ((0, 128),)),
        "green_virt": noise(seeds[4], (NAO, NAO), NAO ** -0.5, 0.125, ((0, 128),)),
    }


def reference(three_center, neighbors, block_sizes, green_occ, green_virt):
    position = jnp.arange(BS, dtype=jnp.int32)
    live_blocks = (position[None, :] < block_sizes[:, None]).astype(jnp.float32)
    live_flat = live_blocks.reshape(NAO)
    occ_blocks = green_occ.reshape(NAT, BS, NAO)[neighbors].astype(jnp.float32)
    row_mask = live_blocks[:, None, :, None]
    col_mask = live_blocks[neighbors][:, :, None, :]

    def per_function(slab):
        masked = slab.astype(jnp.float32) * row_mask * col_mask
        first = jnp.einsum("ajik,ajkl->ail", masked, occ_blocks).astype(jnp.bfloat16)
        first = first.reshape(NAO, NAO)
        second = jnp.dot(green_virt, first, preferred_element_type=jnp.float32)
        return second * live_flat[:, None] * live_flat[None, :]

    return lax.map(per_function, three_center)
```

```python
import functools

import jax
import jax.numpy as jnp
from jax import lax
from jax.experimental import pallas as pl
from jax.experimental.pallas import tpu as pltpu
from jax.sharding import PartitionSpec as P

AXES = ("ri", "ao")
GROUPS = 2
VMEM_LIMIT = 56 * 1024 * 1024
VMEM = pl.BlockSpec(memory_space=pltpu.VMEM)
SMEM = pl.BlockSpec(memory_space=pltpu.SMEM)
ANY = pl.BlockSpec(memory_space=pl.ANY)


def pairs(step):
    out = []
    for z in range(4):
        for y in range(4):
            for x in range(4):
                for c in range(2):
                    tz, ty, tx, tc = step(z, y, x, c)
                    target = (((tz % 4) * 4 + ty % 4) * 4 + tx % 4) * 2 + tc
                    out.append((((z * 4 + y) * 4 + x) * 2 + c, target))
    return out


CORE = pairs(lambda z, y, x, c: (z, y, x, 1 - c))
RING_X = pairs(lambda z, y, x, c: (z, y, x + 1 - 2 * c, c))
SHIFT_X = [None] + [pairs(lambda z, y, x, c, d=d: (z, y, x + d, c)) for d in (1, 2, 3)]
STAGE_A = [None] + [
    pairs(lambda z, y, x, c, d=d: (z + d * c, y + d * (1 - c), x, c)) for d in (1, 2, 3)
]
STAGE_B = [None] + [
    pairs(lambda z, y, x, c, d=d: (z + d * (1 - c), y + d * c, x, c)) for d in (1, 2, 3)
]


def move(value, perm):
    return lax.ppermute(value, AXES, perm)


def spread(value, stage):
    return [value] + [move(value, stage[d]) for d in (1, 2, 3)]


def first_kernel(group, place, neighbors, *refs):
    chunks, occ_mine, occ_other, keep, send, occ = refs[:4], *refs[4:9]
    z, y, x, c = place[0], place[1], place[2], place[3]
    for far in range(4):
        for near in range(4):
            a_mine = lax.rem(z - jnp.where(c == 0, far, near) + 4, 4) * 4 + lax.rem(
                y - jnp.where(c == 0, near, far) + 4, 4
            )
            a_other = lax.rem(z - jnp.where(c == 0, near, far) + 4, 4) * 4 + lax.rem(
                y - jnp.where(c == 0, far, near) + 4, 4
            )
            for shard in range(4):
                occ[a_mine, pl.ds(pl.multiple_of(shard * 32 + c * 16, 16), 16), :] = occ_mine[
                    far, near, shard
                ]
                row = pl.ds(pl.multiple_of(shard * 32 + (1 - c) * 16, 16), 16)
                occ[a_other, row, 0:256] = occ_other[far, near, shard, :, 256:512]
                occ[a_other, row, 256:512] = occ_other[far, near, shard, :, 0:256]
    for step in range(4):
        at = lax.rem(x + jnp.where(c == 0, 4 - step, step), 4)
        for atom in range(2):
            right = jnp.concatenate(
                [occ[neighbors[at, atom * 4 + j]] for j in range(4)], axis=0
            )
            left = jnp.concatenate(
                [
                    jnp.concatenate([chunks[step][p, atom, j] for j in range(4)], axis=1)
                    for p in range(group)
                ],
                axis=0,
            )
            done = jnp.dot(left, right, preferred_element_type=jnp.float32).astype(jnp.bfloat16)
            for p in range(group):
                rows = pl.ds(atom * 128, 128)
                keep[p, at, rows, :] = done[p * 128 : (p + 1) * 128, :256]
                send[p, at, rows, :] = done[p * 128 : (p + 1) * 128, 256:]


def first_call(group, place, neighbors, chunks, occ_mine, occ_other):
    shape = jax.ShapeDtypeStruct((group, 4, 256, 256), jnp.bfloat16)
    return pl.pallas_call(
        functools.partial(first_kernel, group),
        out_shape=(shape, shape),
        in_specs=[SMEM, SMEM] + [VMEM] * 6,
        out_specs=(VMEM, VMEM),
        scratch_shapes=[pltpu.VMEM((16, 128, 512), jnp.bfloat16)],
        compiler_params=pltpu.CompilerParams(vmem_limit_bytes=VMEM_LIMIT),
        cost_estimate=pl.CostEstimate(
            flops=group * 2 * 1024 * 512 * 512, bytes_accessed=group * 3 * 2**20, transcendentals=0
        ),
    )(place, neighbors, *chunks, occ_mine, occ_other)


def second_kernel(group, base, place, keep, other, *refs):
    pieces, _, out, whole, held, result, in_sems, out_sems = refs[:8], *refs[8:15]
    z, y, c = place[0], place[1], place[3]
    total = 8

    def fetch(i):
        return pltpu.make_async_copy(pieces[i], held.at[i % 2], in_sems.at[i % 2])

    def stores(i):
        far, core = i % 4, c if i < 4 else 1 - c
        copies = []
        for near in range(4):
            block = lax.rem(z - jnp.where(core == 0, far, near) + 4, 4) * 4 + lax.rem(
                y - jnp.where(core == 0, near, far) + 4, 4
            )
            copies.append(
                pltpu.make_async_copy(
                    result.at[i % 2, :, near],
                    out.at[pl.ds(base, group), block, :, core],
                    out_sems.at[i % 2, near],
                )
            )
        return copies

    fetch(0).start()
    for shard in range(4):
        for p in range(group):
            whole[p, pl.ds(pl.multiple_of((shard * 2 + c) * 256, 256), 256), :] = keep[p, shard]
            whole[p, pl.ds(pl.multiple_of((shard * 2 + 1 - c) * 256, 256), 256), :] = other[p, shard]
    for i in range(total):
        if i + 1 < total:
            fetch(i + 1).start()
        fetch(i).wait()
        if i >= 2:
            for copy in stores(i - 2):
                copy.wait()
        for p in range(group):
            done = jnp.dot(held[i % 2], whole[p], preferred_element_type=jnp.float32)
            result[i % 2, p] = done.reshape(4, 4, 16, 256)
        for copy in stores(i):
            copy.start()
    for i in (total - 2, total - 1):
        for copy in stores(i):
            copy.wait()


def second_call(group, base, place, keep, other, pieces, out):
    return pl.pallas_call(
        functools.partial(second_kernel, group, base),
        out_shape=jax.ShapeDtypeStruct(out.shape, out.dtype),
        in_specs=[SMEM] + [VMEM] * 2 + [ANY] * 9,
        out_specs=ANY,
        scratch_shapes=[
            pltpu.VMEM((group, 2048, 256), jnp.bfloat16),
            pltpu.VMEM((2, 256, 2048), jnp.bfloat16),
            pltpu.VMEM((2, group, 4, 4, 16, 256), jnp.float32),
            pltpu.SemaphoreType.DMA((2,)),
            pltpu.SemaphoreType.DMA((2, 4)),
        ],
        input_output_aliases={11: 0},
        compiler_params=pltpu.CompilerParams(vmem_limit_bytes=VMEM_LIMIT),
        cost_estimate=pl.CostEstimate(
            flops=group * 2 * 2048 * 2048 * 256,
            bytes_accessed=(8 + group * 3) * 2**20,
            transcendentals=0,
        ),
    )(place, keep, other, *pieces, out)


def blank_kernel(out):
    pass


def blank(shape, dtype):
    return pl.pallas_call(
        blank_kernel, out_shape=jax.ShapeDtypeStruct(shape, dtype), out_specs=ANY
    )()


def body(three_center, neighbors, block_sizes, green_occ, green_virt):
    ri, ao = lax.axis_index("ri"), lax.axis_index("ao")
    z, y, x, c = ri // 4, ri % 4, ao // 2, ao % 2
    place = jnp.stack([z, y, x, c]).astype(jnp.int32)
    group = three_center.shape[0] // GROUPS

    position = jnp.arange(128, dtype=jnp.int32)
    live = (position[None, :] < block_sizes[:, None]).astype(jnp.bfloat16).reshape(2048)
    live_rows = lax.dynamic_slice_in_dim(live, (ri * 8 + ao) * 16, 16, 0)
    mask = live_rows[:, None] * live[None, :]
    occ = green_occ * mask
    virt = green_virt * mask
    near = jnp.zeros((16, 128), jnp.bfloat16).at[0, :8].set(
        neighbors.reshape(8).astype(jnp.bfloat16)
    )

    def pack(d):
        to = lax.rem(x + d, 4) * 512
        mine = lax.dynamic_slice_in_dim(occ, to + c * 256, 256, 1)
        other = lax.dynamic_slice_in_dim(occ, to + (1 - c) * 256, 256, 1)
        return jnp.concatenate([virt, mine, other, near], axis=1)

    packs = [pack(0)] + [move(pack((4 - t) % 4), SHIFT_X[4 - t]) for t in (1, 2, 3)]
    packs = lax.dynamic_slice_in_dim(jnp.stack(packs + packs[:3]), lax.rem(4 - x, 4), 4, 0)
    near_all = packs[:, 0, 2560:2568].astype(jnp.int32)

    occ_a = jnp.stack(spread(packs[:, :, 2048:2560], STAGE_A))
    occ_mine = jnp.stack(spread(occ_a, STAGE_B))
    occ_other = move(occ_mine, CORE)

    virt_a = jnp.concatenate(spread(packs[:, :, :2048].reshape(64, 2048), STAGE_A))
    virt_mine = spread(virt_a, STAGE_B)
    virt_pieces = virt_mine + [move(v, CORE) for v in virt_mine]

    rounds = [[three_center[g * group : (g + 1) * group] for g in range(GROUPS)]]
    for _ in range(3):
        rounds.append([move(piece, RING_X) for piece in rounds[-1]])

    out = blank((64 // 16, 16, 4, 2, 16, 256), jnp.float32)
    for g in range(GROUPS):
        keep, send = first_call(
            group, place, near_all, [r[g] for r in rounds], occ_mine, occ_other
        )
        out = second_call(group, g * group, place, keep, move(send, CORE), virt_pieces, out)
    return out.reshape(4, 2048, 256)


def solution(mesh):
    in_specs = (
        P("ri", "ao", None, None, None),
        P("ao", None),
        P(),
        P(("ri", "ao"), None),
        P(("ri", "ao"), None),
    )
    out_specs = P("ri", None, "ao")
    return jax.shard_map(body, mesh=mesh, in_specs=in_specs, out_specs=out_specs, check_vma=False)
```

```python
import jax
import jax.numpy as jnp
from jax import lax
from jax.experimental import pallas as pl
from jax.experimental.pallas import tpu as pltpu
from jax.sharding import PartitionSpec as P

AXES = ("ri", "ao")
VMEM_LIMIT = 56 * 1024 * 1024
SMEM = pl.BlockSpec(memory_space=pltpu.SMEM)
ANY = pl.BlockSpec(memory_space=pl.ANY)


def pairs(step):
    out = []
    for z in range(4):
        for y in range(4):
            for x in range(4):
                for c in range(2):
                    tz, ty, tx, tc = step(z, y, x, c)
                    target = (((tz % 4) * 4 + ty % 4) * 4 + tx % 4) * 2 + tc
                    out.append((((z * 4 + y) * 4 + x) * 2 + c, target))
    return out


CORE = pairs(lambda z, y, x, c: (z, y, x, 1 - c))
RING_X = pairs(lambda z, y, x, c: (z, y, x + 1 - 2 * c, c))
SHIFT_X = [None] + [pairs(lambda z, y, x, c, d=d: (z, y, x + d, c)) for d in (1, 2, 3)]
STAGE_A = [None] + [
    pairs(lambda z, y, x, c, d=d: (z + d * c, y + d * (1 - c), x, c)) for d in (1, 2, 3)
]
STAGE_B = [None] + [
    pairs(lambda z, y, x, c, d=d: (z + d * (1 - c), y + d * c, x, c)) for d in (1, 2, 3)
]
AHEAD, PACE = 3, 2
KINDS = tuple((far, mine) for far in (0, 1, 3, 2) for mine in (True, False))


def move(value, perm):
    return lax.ppermute(value, AXES, perm)


def spread(value, stage):
    return [value] + [move(value, stage[d]) for d in (1, 2, 3)]


def after(value, *earlier):
    return lax.optimization_barrier((value,) + earlier)[0]


def kernel(place, near, *refs):
    mine_chunks, other_chunks, refs = refs[:4], refs[4:8], refs[8:]
    sources = [
        [(r[0], 0), (r[0], 160)] + [(r[1], 0), (r[1], 160)] + [(r[2], 0), (r[3], 0)] + [(r[4], 0), (r[4], 160)]
        for r in (refs[:5], refs[5:10])
    ]
    mine, other = [[src[2 * far : 2 * far + 2] for far in range(4)] for src in sources]
    out, chunks, occ_in, occ, first, held, result, chunk_sems, occ_sems, in_sems, out_sems = refs[10:]
    z, y, x, c = place[0], place[1], place[2], place[3]

    def block(core, far, b):
        return ((z - jnp.where(core == 0, far, b)) & 3) * 4 + ((y - jnp.where(core == 0, b, far)) & 3)

    blocks = [
        pltpu.make_async_copy((mine_chunks + other_chunks)[i], chunks.at[i], chunk_sems.at[i])
        for i in range(8)
    ]
    greens, fetches = [], []
    for far in range(4):
        for h, (ref, top) in enumerate(mine[far]):
            greens.append(
                pltpu.make_async_copy(
                    ref.at[pl.ds(top + 128, 32)], occ_in.at[far, pl.ds(h * 32, 32)], occ_sems.at[far, h]
                )
            )
    for i, (far, own) in enumerate(KINDS):
        fetches.append(
            [
                pltpu.make_async_copy(
                    ref.at[pl.ds(top, 128)], held.at[i, pl.ds(h * 128, 128)], in_sems.at[i, h]
                )
                for h, (ref, top) in enumerate((mine if own else other)[far])
            ]
        )
    queue = [[copy] for copy in blocks] + fetches

    def ask(count):
        for _ in range(min(count, len(queue))):
            for copy in queue.pop(0):
                copy.start()

    for copy in greens:
        copy.start()
    ask(AHEAD)

    for far in range(4):
        for copy in greens[2 * far : 2 * far + 2]:
            copy.wait()
        for b in range(4):
            at = block(c, far, b)
            for g in range(8):
                occ[at, g * 16 : (g + 1) * 16, :] = occ_in[
                    far, b * 16 : (b + 1) * 16, g * 256 : (g + 1) * 256
                ]

    for i in range(8):
        core = c if i < 4 else 1 - c
        at = (x + jnp.where(core == 0, -(i % 4), i % 4)) & 3
        blocks[i].wait()
        ask(PACE if i % 2 else 1)
        for atom in range(2):
            right = jnp.concatenate(
                [occ[near[at, core * 8 + atom * 4 + j]] for j in range(4)], axis=0
            )
            left = jnp.concatenate(
                [
                    jnp.concatenate([chunks[i, p, atom, j] for j in range(4)], axis=1)
                    for p in range(4)
                ],
                axis=0,
            )
            done = jnp.dot(left, right, preferred_element_type=jnp.float32).astype(jnp.bfloat16)
            rows = pl.ds(pl.multiple_of((core * 4 + at) * 256 + atom * 128, 128), 128)
            for p in range(4):
                first[p, rows, :] = done[p * 128 : (p + 1) * 128]

    def stores(i):
        far, own = KINDS[i]
        core = c if own else 1 - c
        return [
            pltpu.make_async_copy(
                result.at[i % 2, :, b], out.at[:, block(core, far, b), :, core], out_sems.at[i % 2, b]
            )
            for b in range(4)
        ]

    for i in range(8):
        for copy in fetches[i]:
            copy.wait()
        ask(1)
        if i >= 2:
            for copy in stores(i - 2):
                copy.wait()
        for p in range(4):
            done = jnp.dot(held[i], first[p], preferred_element_type=jnp.float32)
            result[i % 2, p] = done.reshape(4, 4, 16, 256)
        for copy in stores(i):
            copy.start()
    for i in (6, 7):
        for copy in stores(i):
            copy.wait()


def contract(place, near, mine_chunks, other_chunks, mine, other):
    return pl.pallas_call(
        kernel,
        out_shape=jax.ShapeDtypeStruct((4, 16, 4, 2, 16, 256), jnp.float32),
        in_specs=[SMEM, SMEM] + [ANY] * 18,
        out_specs=ANY,
        scratch_shapes=[
            pltpu.VMEM((8, 4, 2, 4, 128, 128), jnp.bfloat16),
            pltpu.VMEM((4, 64, 2048), jnp.bfloat16),
            pltpu.VMEM((16, 128, 256), jnp.bfloat16),
            pltpu.VMEM((4, 2048, 256), jnp.bfloat16),
            pltpu.VMEM((8, 256, 2048), jnp.bfloat16),
            pltpu.VMEM((2, 4, 4, 4, 16, 256), jnp.float32),
            pltpu.SemaphoreType.DMA((8,)),
            pltpu.SemaphoreType.DMA((4, 2)),
            pltpu.SemaphoreType.DMA((8, 2)),
            pltpu.SemaphoreType.DMA((2, 4)),
        ],
        compiler_params=pltpu.CompilerParams(vmem_limit_bytes=VMEM_LIMIT),
        cost_estimate=pl.CostEstimate(
            flops=10 * 2**30, bytes_accessed=26 * 2**20, transcendentals=0
        ),
    )(place, near, *mine_chunks, *other_chunks, *mine, *other)


def body(three_center, neighbors, block_sizes, green_occ, green_virt):
    ri, ao = lax.axis_index("ri"), lax.axis_index("ao")
    z, y, x, c = ri // 4, ri % 4, ao // 2, ao % 2
    place = jnp.stack([z, y, x, c]).astype(jnp.int32)

    position = jnp.arange(128, dtype=jnp.int32)
    live = (position[None, :] < block_sizes[:, None]).astype(jnp.bfloat16).reshape(2048)
    live_rows = lax.dynamic_slice_in_dim(live, (ri * 8 + ao) * 16, 16, 0)
    mask = live_rows[:, None] * live[None, :]
    occ = green_occ * mask
    virt = green_virt * mask

    sides = [
        jnp.concatenate([occ[:, b * 512 + k * 256 : b * 512 + k * 256 + 256] for b in range(4)], axis=1)
        for k in range(2)
    ]
    near = lax.dynamic_update_slice(
        jnp.zeros((16, 128), jnp.bfloat16), neighbors.reshape(1, 8).astype(jnp.bfloat16), (0, c * 8)
    )
    own, away = jnp.where(c == 0, sides[0], sides[1]), jnp.where(c == 0, sides[1], sides[0])
    swapped = move(jnp.concatenate([away, near], axis=1), CORE)
    near = near + swapped[:, 1024:]
    rows = [
        jnp.where(c == 0, own, swapped[:, :1024]),
        jnp.where(c == 0, swapped[:, :1024], own),
    ]
    virt = jnp.concatenate(
        [virt[:, b * 512 + k * 256 : b * 512 + k * 256 + 256] for k in range(2) for b in range(4)], axis=1
    )

    def pack(d):
        to = lax.rem(x + d, 4) * 256
        return jnp.concatenate(
            [virt] + [lax.dynamic_slice_in_dim(r, to, 256, 1) for r in rows] + [near], axis=1
        )

    arrived = [pack(0)] + [move(pack((4 - t) % 4), SHIFT_X[4 - t]) for t in (1, 2, 3)]
    packs = lax.dynamic_slice_in_dim(jnp.stack(arrived + arrived[:3]), lax.rem(4 - x, 4), 4, 0)
    near = packs[:, 0, 2560:2576].astype(jnp.int32)

    greens = jnp.concatenate(
        [packs[:, :, :2048].reshape(64, 2048)]
        + [jnp.concatenate([packs[b, :, 2048:2560] for b in range(4)], axis=1)]
    )
    chunks = [three_center]
    other_chunks = [move(three_center, CORE)]
    first_other = other_chunks[0]
    chunks.append(move(after(three_center, arrived[1]), RING_X))
    other_chunks.append(move(chunks[1], CORE))
    chunks.append(move(chunks[1], RING_X))
    other_chunks.append(move(chunks[2], CORE))
    greens = spread(after(greens, other_chunks[0]), STAGE_A)
    greens = jnp.concatenate(
        [g[rows] for pair in (greens[:2], greens[2:]) for rows in (slice(0, 64), slice(64, 80)) for g in pair]
    )
    first_green = move(greens, CORE)
    chunks.append(move(after(chunks[2], other_chunks[1], first_green), RING_X))
    other_chunks.append(move(chunks[3], CORE))
    up, down = move(greens, STAGE_B[1]), move(greens, STAGE_B[3])
    beyond = [move(up[:160], STAGE_B[1]), move(down[160:], STAGE_B[3])]
    mine = [greens, up] + beyond + [down]
    other = [first_green] + [move(after(up, other_chunks[2]), CORE)] + [move(b, CORE) for b in beyond] + [move(after(down, other_chunks[2]), CORE)]

    return contract(place, near, chunks, other_chunks, mine, other).reshape(4, 2048, 256)


def solution(mesh):
    in_specs = (
        P("ri", "ao", None, None, None),
        P("ao", None),
        P(),
        P(("ri", "ao"), None),
        P(("ri", "ao"), None),
    )
    out_specs = P("ri", None, "ao")
    return jax.shard_map(body, mesh=mesh, in_specs=in_specs, out_specs=out_specs, check_vma=False)
```

```python
import jax
import jax.numpy as jnp
from jax import lax
from jax.experimental import pallas as pl
from jax.experimental.pallas import tpu as pltpu
from jax.sharding import PartitionSpec as P

AXES = ("ri", "ao")
VMEM_LIMIT = 56 * 1024 * 1024
SMEM = pl.BlockSpec(memory_space=pltpu.SMEM)
ANY = pl.BlockSpec(memory_space=pl.ANY)


def pairs(step):
    out = []
    for z in range(4):
        for y in range(4):
            for x in range(4):
                for c in range(2):
                    tz, ty, tx, tc = step(z, y, x, c)
                    target = (((tz % 4) * 4 + ty % 4) * 4 + tx % 4) * 2 + tc
                    out.append((((z * 4 + y) * 4 + x) * 2 + c, target))
    return out


CORE = pairs(lambda z, y, x, c: (z, y, x, 1 - c))
RING_X = pairs(lambda z, y, x, c: (z, y, x + 1 - 2 * c, c))
SHIFT_X = [None] + [pairs(lambda z, y, x, c, d=d: (z, y, x + d, c)) for d in (1, 2, 3)]
STAGE_A = [None] + [
    pairs(lambda z, y, x, c, d=d: (z + d * c, y + d * (1 - c), x, c)) for d in (1, 2, 3)
]
STAGE_B = [None] + [
    pairs(lambda z, y, x, c, d=d: (z + d * (1 - c), y + d * c, x, c)) for d in (1, 2, 3)
]
AHEAD, PACE = 3, 2
KINDS = tuple((far, mine) for far in (0, 1, 3, 2) for mine in (True, False))


def move(value, perm):
    return lax.ppermute(value, AXES, perm)


def spread(value, stage):
    return [value] + [move(value, stage[d]) for d in (1, 2, 3)]


def after(value, *earlier):
    return lax.optimization_barrier((value,) + earlier)[0]


def kernel(place, near, *refs):
    mine_chunks, other_chunks, refs = refs[:4], refs[4:8], refs[8:]
    sources = [
        [(r[0], 0), (r[0], 160)] + [(ref, 0) for ref in r[1:]] for r in (refs[:7], refs[7:14])
    ]
    mine, other = [[src[2 * far : 2 * far + 2] for far in range(4)] for src in sources]
    out, chunks, occ_in, occ, first, held, result, chunk_sems, occ_sems, in_sems, out_sems = refs[14:]
    z, y, x, c = place[0], place[1], place[2], place[3]

    def block(core, far, b):
        return ((z - jnp.where(core == 0, far, b)) & 3) * 4 + ((y - jnp.where(core == 0, b, far)) & 3)

    blocks = [
        pltpu.make_async_copy((mine_chunks + other_chunks)[i], chunks.at[i], chunk_sems.at[i])
        for i in range(8)
    ]
    greens, fetches = [], []
    for far in range(4):
        for h, (ref, top) in enumerate(mine[far]):
            greens.append(
                pltpu.make_async_copy(
                    ref.at[pl.ds(top + 128, 32)], occ_in.at[far, pl.ds(h * 32, 32)], occ_sems.at[far, h]
                )
            )
    for i, (far, own) in enumerate(KINDS):
        fetches.append(
            [
                pltpu.make_async_copy(
                    ref.at[pl.ds(top, 128)], held.at[i, pl.ds(h * 128, 128)], in_sems.at[i, h]
                )
                for h, (ref, top) in enumerate((mine if own else other)[far])
            ]
        )
    queue = [[copy] for copy in blocks] + fetches

    def ask(count):
        for _ in range(min(count, len(queue))):
            for copy in queue.pop(0):
                copy.start()

    for copy in greens:
        copy.start()
    ask(AHEAD)

    for far in range(4):
        for copy in greens[2 * far : 2 * far + 2]:
            copy.wait()
        for b in range(4):
            at = block(c, far, b)
            for g in range(8):
                occ[at, g * 16 : (g + 1) * 16, :] = occ_in[
                    far, b * 16 : (b + 1) * 16, g * 256 : (g + 1) * 256
                ]

    for i in range(8):
        core = c if i < 4 else 1 - c
        at = (x + jnp.where(core == 0, -(i % 4), i % 4)) & 3
        blocks[i].wait()
        ask(PACE if i % 2 else 1)
        for atom in range(2):
            right = jnp.concatenate(
                [occ[near[at, core * 8 + atom * 4 + j]] for j in range(4)], axis=0
            )
            left = jnp.concatenate(
                [
                    jnp.concatenate([chunks[i, p, atom, j] for j in range(4)], axis=1)
                    for p in range(4)
                ],
                axis=0,
            )
            done = jnp.dot(left, right, preferred_element_type=jnp.float32).astype(jnp.bfloat16)
            rows = pl.ds(pl.multiple_of((core * 4 + at) * 256 + atom * 128, 128), 128)
            for p in range(4):
                first[p, rows, :] = done[p * 128 : (p + 1) * 128]

    def stores(i):
        far, own = KINDS[i]
        core = c if own else 1 - c
        return [
            pltpu.make_async_copy(
                result.at[i % 2, :, b], out.at[:, block(core, far, b), :, core], out_sems.at[i % 2, b]
            )
            for b in range(4)
        ]

    for i in range(8):
        for copy in fetches[i]:
            copy.wait()
        ask(1)
        if i >= 2:
            for copy in stores(i - 2):
                copy.wait()
        for p in range(4):
            done = jnp.dot(held[i], first[p], preferred_element_type=jnp.float32)
            result[i % 2, p] = done.reshape(4, 4, 16, 256)
        for copy in stores(i):
            copy.start()
    for i in (6, 7):
        for copy in stores(i):
            copy.wait()


def contract(place, near, mine_chunks, other_chunks, mine, other):
    return pl.pallas_call(
        kernel,
        out_shape=jax.ShapeDtypeStruct((4, 16, 4, 2, 16, 256), jnp.float32),
        in_specs=[SMEM, SMEM] + [ANY] * 22,
        out_specs=ANY,
        scratch_shapes=[
            pltpu.VMEM((8, 4, 2, 4, 128, 128), jnp.bfloat16),
            pltpu.VMEM((4, 64, 2048), jnp.bfloat16),
            pltpu.VMEM((16, 128, 256), jnp.bfloat16),
            pltpu.VMEM((4, 2048, 256), jnp.bfloat16),
            pltpu.VMEM((8, 256, 2048), jnp.bfloat16),
            pltpu.VMEM((2, 4, 4, 4, 16, 256), jnp.float32),
            pltpu.SemaphoreType.DMA((8,)),
            pltpu.SemaphoreType.DMA((4, 2)),
            pltpu.SemaphoreType.DMA((8, 2)),
            pltpu.SemaphoreType.DMA((2, 4)),
        ],
        compiler_params=pltpu.CompilerParams(vmem_limit_bytes=VMEM_LIMIT),
        cost_estimate=pl.CostEstimate(
            flops=10 * 2**30, bytes_accessed=26 * 2**20, transcendentals=0
        ),
    )(place, near, *mine_chunks, *other_chunks, *mine, *other)


def body(three_center, neighbors, block_sizes, green_occ, green_virt):
    ri, ao = lax.axis_index("ri"), lax.axis_index("ao")
    z, y, x, c = ri // 4, ri % 4, ao // 2, ao % 2
    place = jnp.stack([z, y, x, c]).astype(jnp.int32)

    position = jnp.arange(128, dtype=jnp.int32)
    live = (position[None, :] < block_sizes[:, None]).astype(jnp.bfloat16).reshape(2048)
    live_rows = lax.dynamic_slice_in_dim(live, (ri * 8 + ao) * 16, 16, 0)
    mask = live_rows[:, None] * live[None, :]
    occ = green_occ * mask
    virt = green_virt * mask

    sides = [
        jnp.concatenate([occ[:, b * 512 + k * 256 : b * 512 + k * 256 + 256] for b in range(4)], axis=1)
        for k in range(2)
    ]
    near = lax.dynamic_update_slice(
        jnp.zeros((16, 128), jnp.bfloat16), neighbors.reshape(1, 8).astype(jnp.bfloat16), (0, c * 8)
    )
    own, away = jnp.where(c == 0, sides[0], sides[1]), jnp.where(c == 0, sides[1], sides[0])
    swapped = move(jnp.concatenate([away, near], axis=1), CORE)
    near = near + swapped[:, 1024:]
    rows = [
        jnp.where(c == 0, own, swapped[:, :1024]),
        jnp.where(c == 0, swapped[:, :1024], own),
    ]
    virt = jnp.concatenate(
        [virt[:, b * 512 + k * 256 : b * 512 + k * 256 + 256] for k in range(2) for b in range(4)], axis=1
    )

    def pack(d):
        to = lax.rem(x + d, 4) * 256
        return jnp.concatenate(
            [virt] + [lax.dynamic_slice_in_dim(r, to, 256, 1) for r in rows] + [near], axis=1
        )

    packed = lax.optimization_barrier(tuple(pack((4 - t) % 4) for t in range(4)))
    arrived = [packed[0]] + [move(packed[t], SHIFT_X[4 - t]) for t in (1, 2, 3)]
    packs = lax.dynamic_slice_in_dim(jnp.stack(arrived + arrived[:3]), lax.rem(4 - x, 4), 4, 0)
    near = packs[:, 0, 2560:2576].astype(jnp.int32)

    greens = jnp.concatenate(
        [packs[:, :, :2048].reshape(64, 2048)]
        + [jnp.concatenate([packs[b, :, 2048:2560] for b in range(4)], axis=1)]
    )
    greens = jnp.concatenate(
        [packs[:, :, :2048].reshape(64, 2048)]
        + [jnp.concatenate([packs[b, :, 2048:2560] for b in range(4)], axis=1)]
    )
    chunks = [three_center]
    c_m = [move(three_center, CORE)]
    chunks.append(move(after(three_center, *packed), RING_X))
    c_m.append(move(chunks[1], CORE))
    chunks.append(move(chunks[1], RING_X))

    greens = spread(after(greens, c_m[0]), STAGE_A)
    greens = lax.optimization_barrier(tuple(greens))
    halves = [
        jnp.concatenate([g[:64] for g in pair] + [g[64:] for g in pair])
        for pair in (greens[:2], greens[2:])
    ]
    whole = jnp.concatenate(halves)
    c_w = move(whole, CORE)
    chunks.append(move(after(chunks[2], c_w), RING_X))
    up0, down1 = move(halves[0], STAGE_B[1]), move(halves[1], STAGE_B[3])
    c_m.append(move(chunks[2], CORE))
    up1, down0 = [move(after(h, c_m[1], c_w), STAGE_B[d]) for h, d in ((halves[1], 1), (halves[0], 3))]
    c_u0 = move(after(up0, c_m[2]), CORE)
    c_d1 = move(after(down1, c_u0), CORE)
    b0, b1 = move(up0, STAGE_B[1]), move(down1, STAGE_B[3])
    c_u1 = move(after(up1, c_m[2]), CORE)
    c_d0 = move(down0, CORE)
    c_b0 = move(after(b0, c_m[2]), CORE)
    c_b1 = move(after(b1, c_m[2]), CORE)
    c_m.append(move(chunks[3], CORE))
    other_chunks = c_m
    mine = [whole, up0, up1, b0, b1, down0, down1]
    other = [c_w, c_u0, c_u1, c_b0, c_b1, c_d0, c_d1]

    return contract(place, near, chunks, other_chunks, mine, other).reshape(4, 2048, 256)


def solution(mesh):
    in_specs = (
        P("ri", "ao", None, None, None),
        P("ao", None),
        P(),
        P(("ri", "ao"), None),
        P(("ri", "ao"), None),
    )
    out_specs = P("ri", None, "ao")
    return jax.shard_map(body, mesh=mesh, in_specs=in_specs, out_specs=out_specs, check_vma=False)
```

```python
import jax
import jax.numpy as jnp
from jax import lax
from jax.experimental import pallas as pl
from jax.experimental.pallas import tpu as pltpu
from jax.sharding import PartitionSpec as P

AXES = ("ri", "ao")
VMEM_LIMIT = 56 * 1024 * 1024
SMEM = pl.BlockSpec(memory_space=pltpu.SMEM)
ANY = pl.BlockSpec(memory_space=pl.ANY)


def pairs(step):
    out = []
    for z in range(4):
        for y in range(4):
            for x in range(4):
                for c in range(2):
                    tz, ty, tx, tc = step(z, y, x, c)
                    target = (((tz % 4) * 4 + ty % 4) * 4 + tx % 4) * 2 + tc
                    out.append((((z * 4 + y) * 4 + x) * 2 + c, target))
    return out


CORE = pairs(lambda z, y, x, c: (z, y, x, 1 - c))
RING_X = pairs(lambda z, y, x, c: (z, y, x + 1 - 2 * c, c))
SHIFT_X = [None] + [pairs(lambda z, y, x, c, d=d: (z, y, x + d, c)) for d in (1, 2, 3)]
STAGE_A = [None] + [
    pairs(lambda z, y, x, c, d=d: (z + d * c, y + d * (1 - c), x, c)) for d in (1, 2, 3)
]
STAGE_B = [None] + [
    pairs(lambda z, y, x, c, d=d: (z + d * (1 - c), y + d * c, x, c)) for d in (1, 2, 3)
]
AHEAD, PACE = 4, 2
KINDS = tuple((far, mine) for far in (0, 1, 3, 2) for mine in (True, False))


def move(value, perm):
    return lax.ppermute(value, AXES, perm)


def spread(value, stage):
    return [value] + [move(value, stage[d]) for d in (1, 2, 3)]


def after(value, *earlier):
    return lax.optimization_barrier((value,) + earlier)[0]


def kernel(place, near, *refs):
    mine_chunks, other_chunks, refs = refs[:4], refs[4:8], refs[8:]
    sources = [
        [(r[0], 0), (r[0], 160)] + [(ref, 0) for ref in r[1:]] for r in (refs[:7], refs[7:14])
    ]
    mine, other = [[src[2 * far : 2 * far + 2] for far in range(4)] for src in sources]
    out, chunks, occ_in, occ, first, held, result, chunk_sems, occ_sems, in_sems, out_sems = refs[14:]
    z, y, x, c = place[0], place[1], place[2], place[3]

    def block(core, far, b):
        return ((z - jnp.where(core == 0, far, b)) & 3) * 4 + ((y - jnp.where(core == 0, b, far)) & 3)

    blocks = [
        pltpu.make_async_copy((mine_chunks + other_chunks)[i], chunks.at[i], chunk_sems.at[i])
        for i in range(8)
    ]
    greens, fetches = [], []
    for far in range(4):
        for h, (ref, top) in enumerate(mine[far]):
            greens.append(
                pltpu.make_async_copy(
                    ref.at[pl.ds(top + 128, 32)], occ_in.at[far, pl.ds(h * 32, 32)], occ_sems.at[far, h]
                )
            )
    for i, (far, own) in enumerate(KINDS):
        fetches.append(
            [
                pltpu.make_async_copy(
                    ref.at[pl.ds(top, 128)], held.at[i, pl.ds(h * 128, 128)], in_sems.at[i, h]
                )
                for h, (ref, top) in enumerate((mine if own else other)[far])
            ]
        )
    queue = [[copy] for copy in blocks] + fetches

    def ask(count):
        for _ in range(min(count, len(queue))):
            for copy in queue.pop(0):
                copy.start()

    for copy in greens:
        copy.start()
    ask(AHEAD)

    for far in range(4):
        for copy in greens[2 * far : 2 * far + 2]:
            copy.wait()
        for b in range(4):
            at = block(c, far, b)
            for g in range(8):
                occ[at, g * 16 : (g + 1) * 16, :] = occ_in[
                    far, b * 16 : (b + 1) * 16, g * 256 : (g + 1) * 256
                ]

    for i in range(8):
        core = c if i < 4 else 1 - c
        at = (x + jnp.where(core == 0, -(i % 4), i % 4)) & 3
        blocks[i].wait()
        ask(PACE if i % 2 else 1)
        for atom in range(2):
            right = jnp.concatenate(
                [occ[near[at, core * 8 + atom * 4 + j]] for j in range(4)], axis=0
            )
            left = jnp.concatenate(
                [
                    jnp.concatenate([chunks[i, p, atom, j] for j in range(4)], axis=1)
                    for p in range(4)
                ],
                axis=0,
            )
            done = jnp.dot(left, right, preferred_element_type=jnp.float32).astype(jnp.bfloat16)
            rows = pl.ds(pl.multiple_of((core * 4 + at) * 256 + atom * 128, 128), 128)
            for p in range(4):
                first[p, rows, :] = done[p * 128 : (p + 1) * 128]

    def stores(i):
        far, own = KINDS[i]
        core = c if own else 1 - c
        return [
            pltpu.make_async_copy(
                result.at[i % 2, :, b], out.at[:, block(core, far, b), :, core], out_sems.at[i % 2, b]
            )
            for b in range(4)
        ]

    for i in range(8):
        for copy in fetches[i]:
            copy.wait()
        ask(1)
        if i >= 2:
            for copy in stores(i - 2):
                copy.wait()
        for p in range(4):
            done = jnp.dot(held[i], first[p], preferred_element_type=jnp.float32)
            result[i % 2, p] = done.reshape(4, 4, 16, 256)
        for copy in stores(i):
            copy.start()
    for i in (6, 7):
        for copy in stores(i):
            copy.wait()


def contract(place, near, mine_chunks, other_chunks, mine, other):
    return pl.pallas_call(
        kernel,
        out_shape=jax.ShapeDtypeStruct((4, 16, 4, 2, 16, 256), jnp.float32),
        in_specs=[SMEM, SMEM] + [ANY] * 22,
        out_specs=ANY,
        scratch_shapes=[
            pltpu.VMEM((8, 4, 2, 4, 128, 128), jnp.bfloat16),
            pltpu.VMEM((4, 64, 2048), jnp.bfloat16),
            pltpu.VMEM((16, 128, 256), jnp.bfloat16),
            pltpu.VMEM((4, 2048, 256), jnp.bfloat16),
            pltpu.VMEM((8, 256, 2048), jnp.bfloat16),
            pltpu.VMEM((2, 4, 4, 4, 16, 256), jnp.float32),
            pltpu.SemaphoreType.DMA((8,)),
            pltpu.SemaphoreType.DMA((4, 2)),
            pltpu.SemaphoreType.DMA((8, 2)),
            pltpu.SemaphoreType.DMA((2, 4)),
        ],
        compiler_params=pltpu.CompilerParams(vmem_limit_bytes=VMEM_LIMIT),
        cost_estimate=pl.CostEstimate(
            flops=10 * 2**30, bytes_accessed=26 * 2**20, transcendentals=0
        ),
    )(place, near, *mine_chunks, *other_chunks, *mine, *other)


def body(three_center, neighbors, block_sizes, green_occ, green_virt):
    ri, ao = lax.axis_index("ri"), lax.axis_index("ao")
    z, y, x, c = ri // 4, ri % 4, ao // 2, ao % 2
    place = jnp.stack([z, y, x, c]).astype(jnp.int32)

    position = jnp.arange(128, dtype=jnp.int32)
    live = (position[None, :] < block_sizes[:, None]).astype(jnp.bfloat16).reshape(2048)
    live_rows = lax.dynamic_slice_in_dim(live, (ri * 8 + ao) * 16, 16, 0)
    mask = live_rows[:, None] * live[None, :]
    occ = green_occ * mask
    virt = green_virt * mask

    sides = [
        jnp.concatenate([occ[:, b * 512 + k * 256 : b * 512 + k * 256 + 256] for b in range(4)], axis=1)
        for k in range(2)
    ]
    near = lax.dynamic_update_slice(
        jnp.zeros((16, 128), jnp.bfloat16), neighbors.reshape(1, 8).astype(jnp.bfloat16), (0, c * 8)
    )
    own, away = jnp.where(c == 0, sides[0], sides[1]), jnp.where(c == 0, sides[1], sides[0])
    swapped = move(jnp.concatenate([away, near], axis=1), CORE)
    near = near + swapped[:, 1024:]
    rows = [
        jnp.where(c == 0, own, swapped[:, :1024]),
        jnp.where(c == 0, swapped[:, :1024], own),
    ]
    virt = jnp.concatenate(
        [virt[:, b * 512 + k * 256 : b * 512 + k * 256 + 256] for k in range(2) for b in range(4)], axis=1
    )

    def pack(d):
        to = lax.rem(x + d, 4) * 256
        return jnp.concatenate(
            [virt] + [lax.dynamic_slice_in_dim(r, to, 256, 1) for r in rows] + [near], axis=1
        )

    packed = lax.optimization_barrier(tuple(pack((4 - t) % 4) for t in range(4)))
    arrived = [packed[0]] + [move(packed[t], SHIFT_X[4 - t]) for t in (1, 2, 3)]
    packs = lax.dynamic_slice_in_dim(jnp.stack(arrived + arrived[:3]), lax.rem(4 - x, 4), 4, 0)
    near = packs[:, 0, 2560:2576].astype(jnp.int32)

    greens = jnp.concatenate(
        [packs[:, :, :2048].reshape(64, 2048)]
        + [jnp.concatenate([packs[b, :, 2048:2560] for b in range(4)], axis=1)]
    )
    greens = jnp.concatenate(
        [packs[:, :, :2048].reshape(64, 2048)]
        + [jnp.concatenate([packs[b, :, 2048:2560] for b in range(4)], axis=1)]
    )
    chunks = [three_center]
    c_m = [move(three_center, CORE)]
    chunks.append(move(after(three_center, *packed), RING_X))
    c_m.append(move(chunks[1], CORE))
    chunks.append(move(chunks[1], RING_X))

    greens = spread(after(greens, c_m[0]), STAGE_A)
    greens = lax.optimization_barrier(tuple(greens))
    halves = [
        jnp.concatenate([g[:64] for g in pair] + [g[64:] for g in pair])
        for pair in (greens[:2], greens[2:])
    ]
    whole = jnp.concatenate(halves)
    c_w = move(whole, CORE)
    chunks.append(move(after(chunks[2], c_w), RING_X))
    up0, down1 = move(halves[0], STAGE_B[1]), move(halves[1], STAGE_B[3])
    c_m.append(move(chunks[2], CORE))
    up1, down0 = [move(after(h, c_m[1], c_w), STAGE_B[d]) for h, d in ((halves[1], 1), (halves[0], 3))]
    c_u0 = move(after(up0, c_m[2]), CORE)
    c_d1 = move(after(down1, c_u0), CORE)
    b0, b1 = move(up0, STAGE_B[1]), move(down1, STAGE_B[3])
    c_u1 = move(after(up1, c_m[2]), CORE)
    c_d0 = move(down0, CORE)
    c_b0 = move(after(b0, c_m[2]), CORE)
    c_b1 = move(after(b1, c_m[2]), CORE)
    c_m.append(move(chunks[3], CORE))
    other_chunks = c_m
    mine = [whole, up0, up1, b0, b1, down0, down1]
    other = [c_w, c_u0, c_u1, c_b0, c_b1, c_d0, c_d1]

    return contract(place, near, chunks, other_chunks, mine, other).reshape(4, 2048, 256)


def solution(mesh):
    in_specs = (
        P("ri", "ao", None, None, None),
        P("ao", None),
        P(),
        P(("ri", "ao"), None),
        P(("ri", "ao"), None),
    )
    out_specs = P("ri", None, "ao")
    return jax.shard_map(body, mesh=mesh, in_specs=in_specs, out_specs=out_specs, check_vma=False)
```
